32 devices in a mesh: grp: 2 (over y), section: 2 (over x), lat: 2 (over core), lon: 4 (over z).
Axes of the slice: x: 2, y: 2, z: 4, core: 2. Of those that a mesh axis runs over, the one named last changes fastest.
Arguments:
- section_input: bfloat16 [2, 64, 32, 1536], P('section', ('grp', 'lat'), 'lon'), parts along dimension 1, may hold values from -6 to 6
- fresh_input: bfloat16 [64, 32, 1536], P(('grp', 'lat'), 'lon'), parts along dimension 0, may hold values from -6 to 6
- offsets: int32 [4], P('grp'), parts along dimension 0, may hold values from 1 to 4, as said below
- regions: int32 [64, 32], P(('grp', 'lat'), 'lon'), parts along dimension 0, may hold values from 0 to 8, as said below
- up_weight: bfloat16 [2, 1536, 3072], P('section', 'lon', 'lat'), may hold values from -0.15625 to 0.15625
- up_bias: float32 [2, 3072], P('section', 'lat'), may hold values from -3 to 3
- down_weight: bfloat16 [2, 3072, 1536], P('section', 'lat', 'lon'), may hold values from -0.109375 to 0.109375
- mlp_gain: float32 [2, 1536], P('section'), may hold values from 0.5 to 1.5
- qkv_weight: bfloat16 [2, 1536, 3, 768], P('section', 'lon', None, 'lat'), may hold values from -0.15625 to 0.15625
- logit_scale: float32 [2, 12], P('section', 'lat'), may hold values from 2 to 20
- position_bias: float32 [2, 12, 64, 64], P('section', 'lat'), may hold values from 0 to 8
- out_weight: bfloat16 [2, 768, 1536], P('section', 'lat', 'lon'), may hold values from -0.21875 to 0.21875
- attn_gain: float32 [2, 1536], P('section'), may hold values from 0.5 to 1.5
Outputs:
- handed: bfloat16 [2, 64, 32, 1536], P('section', ('grp', 'lat'), 'lon'), parts along dimension 1
- opened: bfloat16 [2, 64, 32, 1536], P('section', ('grp', 'lat'), 'lon'), parts along dimension 1
The draws below stay inside these ranges and needn't reach their ends.
There are 2 independent parts, one for each index of `grp`. The reference program is written for one: setup_inputs(seed, part) draws one part's arguments, and reference() takes and returns one part's arrays. A program takes and returns all parts, laid end to end along the dimension named above; an argument that names none is the same for every part. Nothing has to cross between parts.
Inputs may be any that keep to these rules, and one draw needn't show every extreme that they name: offsets[0] is the latitude shift and offsets[1] the longitude shift; at least one of them equals 4. `regions`: the shifted-window region id of each token of the rolled grid: 3 * a + b, where a is 0 for rows i < 24, 1 for 24 <= i < 32 - offsets[0] and 2 for the rest, and b is the same for columns with 32 and offsets[1].
All inputs are finite; a program needn't handle non-finite values.
Results may differ from the reference program's by a relative error of at most 0.014.
Values may be sent and summed in bfloat16 or wider, within the bound.
A program may use at most 64 MiB of HBM per device.

```python
import math
import jax
import jax.numpy as jnp
from jax import lax

D = 1536
HIDDEN_SIZE = 3072
ATT_HEADS = 12
HEAD_DIM = 64
W = 8
SECTIONS = 2
NLAT = 32
NLON = 32
N_LAT = 2


def shift_pair(key):
    key_one, key_two = jax.random.split(jax.random.fold_in(key, 11))
    largest = W // 2
    first = jax.random.randint(key_one, (), 1, largest + 1)
    second = jax.random.randint(key_two, (), 1, largest + 1)
    second = jnp.where(first < largest, largest, second)
    return jnp.stack([first, second]).astype(jnp.int32)


def draw_offsets(key, part):
    return shift_pair(key)


def slab_ids(count, shift):
    place = jnp.arange(count, dtype=jnp.int32)
    middle = (place >= count - W).astype(jnp.int32)
    last = (place >= count - shift).astype(jnp.int32)
    return middle + last


def draw_regions(key, part):
    pair = shift_pair(key)
    lat_slab = slab_ids(NLAT, pair[0])
    lon_slab = slab_ids(NLON, pair[1])
    return (3 * lat_slab[:, None] + lon_slab[None, :]).astype(jnp.int32)


def shard_levels(own_key, extent, cuts, least, top_value):
    loudness = 1.0
    for axis_at, blocks in cuts:
        steps = jax.random.uniform(jax.random.fold_in(jax.random.fold_in(own_key, 6), axis_at), (blocks,), jnp.float32, least / len(cuts), top_value / len(cuts))
        loudness = loudness * jnp.repeat(jnp.exp(steps), extent[axis_at] // blocks).reshape((-1,) + (1,) * (len(extent) - 1 - axis_at))
    return loudness


def gaussian(own_key, dims, scale, most, cuts=(), held_as=jnp.bfloat16):
    array = scale * jax.random.normal(own_key, dims, jnp.float32)
    if cuts:
        array = array * shard_levels(own_key, dims, cuts, -0.22, 0.18)
    return jnp.clip(array, -most, most).astype(held_as)


def setup_inputs(seed: int = 0, part: int = 0) -> dict:
    seeds = jax.random.split(jax.random.key(seed), 14)
    part_splits = jax.random.split(jax.random.fold_in(seeds[13], part), 14)
    section_input = gaussian(part_splits[0], (SECTIONS, NLAT, NLON, D), 1.0, 6.0, ((0, 2), (1, 2), (2, 4)))
    fresh_input = gaussian(part_splits[1], (NLAT, NLON, D), 1.0, 6.0, ((0, 2), (1, 4)))
    offsets = draw_offsets(jax.random.fold_in(jax.random.fold_in(seeds[13], part), 71), part)
    regions = draw_regions(jax.random.fold_in(jax.random.fold_in(seeds[13], part), 71), part)
    up_weight = gaussian(seeds[4], (SECTIONS, D, HIDDEN_SIZE), D ** -0.5, 0.15625, ((0, 2), (1, 4), (2, 2)))
    up_bias = gaussian(seeds[5], (SECTIONS, HIDDEN_SIZE), 0.5, 3.0, ((0, 2), (1, 2)), jnp.float32)
    down_weight = gaussian(seeds[6], (SECTIONS, HIDDEN_SIZE, D), HIDDEN_SIZE ** -0.5, 0.109375, ((0, 2), (1, 2), (2, 4)))
    mlp_gain = jnp.clip(1.0 + 0.1 * jax.random.normal(seeds[7], (SECTIONS, D), jnp.float32), 0.5, 1.5)
    qkv_weight = gaussian(seeds[8], (SECTIONS, D, 3, ATT_HEADS * HEAD_DIM), D ** -0.5, 0.15625, ((0, 2), (1, 4), (3, 2)))
    logit_scale = jnp.clip(jnp.exp(math.log(20.0) - 2.3025851 * jax.random.uniform(seeds[9], (SECTIONS, ATT_HEADS), jnp.float32) ** shard_levels(seeds[9], (SECTIONS, ATT_HEADS), ((0, 2), (1, 2)), -0.2, 0.2)), 2.0, 20.0)
    position_bias = jnp.clip(8.0 * jax.random.uniform(seeds[10], (SECTIONS, ATT_HEADS, W * W, W * W), jnp.float32) ** shard_levels(seeds[10], (SECTIONS, ATT_HEADS, W * W, W * W), ((0, 2), (1, 2)), -0.2, 0.2), 0.0, 8.0)
    out_weight = gaussian(seeds[11], (SECTIONS, ATT_HEADS * HEAD_DIM, D), (ATT_HEADS * HEAD_DIM) ** -0.5, 0.21875, ((0, 2), (1, 2), (2, 4)))
    attn_gain = jnp.clip(1.0 + 0.1 * jax.random.normal(seeds[12], (SECTIONS, D), jnp.float32), 0.5, 1.5)
    return {"section_input": section_input, "fresh_input": fresh_input, "offsets": offsets, "regions": regions, "up_weight": up_weight, "up_bias": up_bias, "down_weight": down_weight, "mlp_gain": mlp_gain, "qkv_weight": qkv_weight, "logit_scale": logit_scale, "position_bias": position_bias, "out_weight": out_weight, "attn_gain": attn_gain}


def layer_norm(total, norm_gain):
    mean = lax.optimization_barrier(jnp.mean(total, axis=-1, keepdims=True))
    centered = total - mean
    variance = lax.optimization_barrier(jnp.mean(centered * centered, axis=-1, keepdims=True))
    return centered * lax.rsqrt(variance + 1e-05) * norm_gain

def windows(values, side):
    height, breadth = (values.shape[0], values.shape[1])
    rest = values.shape[2:]
    blocks = values.reshape((height // side, side, breadth // side, side) + rest)
    blocks = jnp.moveaxis(blocks, 2, 1)
    return blocks.reshape((-1, side * side) + rest)

def unwindow(values, height, breadth, side):
    rest = values.shape[2:]
    blocks = values.reshape((height // side, breadth // side, side, side) + rest)
    blocks = jnp.moveaxis(blocks, 1, 2)
    return blocks.reshape((height, breadth) + rest)

def attend(packed, region_marks, head_scale, pos_bias):
    blocks = windows(packed, W).astype(jnp.float32)
    query_rows = blocks[:, :, 0]
    key_rows = blocks[:, :, 1]
    value_rows = blocks[:, :, 2]
    inner_dot = jnp.einsum('wihd,wjhd->whij', query_rows, key_rows)
    query_norm = lax.rsqrt(lax.optimization_barrier(jnp.sum(query_rows * query_rows, axis=-1)) + 1e-06)
    key_norm = lax.rsqrt(lax.optimization_barrier(jnp.sum(key_rows * key_rows, axis=-1)) + 1e-06)
    cosine = inner_dot * jnp.transpose(query_norm, (0, 2, 1))[:, :, :, None]
    cosine = cosine * jnp.transpose(key_norm, (0, 2, 1))[:, :, None, :]
    score = cosine * head_scale[None, :, None, None] + pos_bias[None]
    marked = windows(region_marks, W)
    same_region = (marked[:, :, None] == marked[:, None, :])[:, None]
    raw_weights = jnp.where(same_region, jnp.exp(score), jnp.float32(0.0))
    weights = (raw_weights / lax.optimization_barrier(jnp.sum(raw_weights, axis=-1, keepdims=True))).astype(jnp.bfloat16)
    context = jnp.einsum('whij,wjhd->wihd', weights.astype(jnp.float32), value_rows)
    return context.astype(jnp.bfloat16)

def block_sum(left, right, parts):
    block = left.shape[1] // parts
    total = jnp.zeros((left.shape[0], right.shape[1]), jnp.float32)
    for index in range(parts):
        term = jnp.dot(left[:, index * block:(index + 1) * block], right[index * block:(index + 1) * block], preferred_element_type=jnp.float32)
        rounded = lax.optimization_barrier(term.astype(jnp.bfloat16))
        total = total + rounded.astype(jnp.float32)
    return total

def reference(section_input, fresh_input, offsets, regions, up_weight, up_bias, down_weight, mlp_gain, qkv_weight, logit_scale, position_bias, out_weight, attn_gain):
    shift_lat = offsets[0]
    shift_lon = offsets[1]
    handed_list = []
    opened_list = []
    entering = fresh_input
    for section in range(SECTIONS):
        flat_rows = section_input[section].reshape(-1, D)
        pre_act = jnp.dot(flat_rows, up_weight[section], preferred_element_type=jnp.float32) + up_bias[section]
        hidden = jax.nn.gelu(pre_act, approximate=False).astype(jnp.bfloat16)
        mlp_sum = block_sum(hidden, down_weight[section], N_LAT)
        handed = (flat_rows.astype(jnp.float32) + layer_norm(mlp_sum, mlp_gain[section])).astype(jnp.bfloat16)
        handed_list.append(handed.reshape(NLAT, NLON, D))
        rolled = jnp.roll(entering, (-shift_lat, -shift_lon), axis=(0, 1))
        packed = jnp.dot(rolled.reshape(-1, D), qkv_weight[section].reshape(D, -1), preferred_element_type=jnp.float32)
        packed = packed.astype(jnp.bfloat16).reshape(NLAT, NLON, 3, ATT_HEADS, HEAD_DIM)
        context = attend(packed, regions, logit_scale[section], position_bias[section])
        context = unwindow(context, NLAT, NLON, W).reshape(NLAT * NLON, ATT_HEADS * HEAD_DIM)
        attn_sum = block_sum(context, out_weight[section], N_LAT)
        branch = layer_norm(attn_sum, attn_gain[section]).astype(jnp.bfloat16).reshape(NLAT, NLON, D)
        branch = jnp.roll(branch, (shift_lat, shift_lon), axis=(0, 1))
        opened = (entering.astype(jnp.float32) + branch.astype(jnp.float32)).astype(jnp.bfloat16)
        opened_list.append(opened)
        entering = handed_list[-1]
    return (jnp.stack(handed_list), jnp.stack(opened_list))
```

```python
import jax
import jax.numpy as jnp
from jax import lax
from jax.sharding import PartitionSpec as P

W = 8


def shifted(array, axis, by):
    count = lax.axis_size(axis)
    pairs = [(i, i + by) for i in range(count) if 0 <= i + by < count]
    return lax.ppermute(array, axis, pairs)


def from_behind(block, axis, distance):
    devices = range(lax.axis_size(axis))
    route = [((i - distance) % len(devices), i) for i in devices]
    return lax.ppermute(block, axis, route)


def layer_norm(total, norm_gain):
    mean = jnp.mean(total, axis=-1, keepdims=True)
    centered = total - mean
    variance = jnp.mean(centered * centered, axis=-1, keepdims=True)
    return centered * lax.rsqrt(variance + 1e-05) * norm_gain


def windows(values, side):
    height, breadth = (values.shape[0], values.shape[1])
    rest = values.shape[2:]
    blocks = values.reshape((height // side, side, breadth // side, side) + rest)
    blocks = jnp.moveaxis(blocks, 2, 1)
    return blocks.reshape((-1, side * side) + rest)


def unwindow(values, height, breadth, side):
    rest = values.shape[2:]
    blocks = values.reshape((height // side, breadth // side, side, side) + rest)
    blocks = jnp.moveaxis(blocks, 1, 2)
    return blocks.reshape((height, breadth) + rest)


def attend(packed, region_marks, head_scale, pos_bias):
    blocks = windows(packed, W)
    query_rows = blocks[:, :, 0]
    key_rows = blocks[:, :, 1]
    value_rows = blocks[:, :, 2]
    inner_dot = jnp.einsum(
        "wihd,wjhd->whij", query_rows, key_rows, preferred_element_type=jnp.float32
    )
    query_wide = query_rows.astype(jnp.float32)
    key_wide = key_rows.astype(jnp.float32)
    query_norm = lax.rsqrt(jnp.sum(query_wide * query_wide, axis=-1) + 1e-06)
    key_norm = lax.rsqrt(jnp.sum(key_wide * key_wide, axis=-1) + 1e-06)
    cosine = inner_dot * jnp.transpose(query_norm, (0, 2, 1))[:, :, :, None]
    cosine = cosine * jnp.transpose(key_norm, (0, 2, 1))[:, :, None, :]
    score = cosine * head_scale[None, :, None, None] + pos_bias[None]
    marked = windows(region_marks, W)
    same_region = (marked[:, :, None] == marked[:, None, :])[:, None]
    raw_weights = jnp.where(same_region, jnp.exp(score), jnp.float32(0.0))
    weights = (raw_weights / jnp.sum(raw_weights, axis=-1, keepdims=True)).astype(jnp.bfloat16)
    context = jnp.einsum("whij,wjhd->wihd", weights, value_rows, preferred_element_type=jnp.float32)
    return context.astype(jnp.bfloat16)


def gather_weight(shard):
    copies = lax.axis_size("grp")
    rows = shard.shape[0] // copies
    part = lax.dynamic_slice_in_dim(shard, lax.axis_index("grp") * rows, rows, 0)
    whole = lax.all_gather(part, ("lon", "grp"), axis=0, tiled=True)
    return whole.reshape((lax.axis_size("lon"),) + shard.shape)


def by_rows(shard):
    whole = gather_weight(shard)
    return whole.reshape((-1,) + shard.shape[1:])


def times_columns(left, shard):
    whole = gather_weight(shard)
    terms = jnp.einsum("th,lhc->tlc", left, whole, preferred_element_type=jnp.float32)
    return terms.reshape(left.shape[0], -1)


def per_device(
    section_input,
    fresh_input,
    offsets,
    regions,
    up_weight,
    up_bias,
    down_weight,
    mlp_gain,
    qkv_weight,
    logit_scale,
    position_bias,
    out_weight,
    attn_gain,
):
    tile_in = section_input[0]
    height, breadth, width = tile_in.shape
    gathered = lax.all_gather(tile_in, "lat", axis=0, tiled=True)
    flat_rows = gathered.reshape(-1, width)
    up_local = up_weight[0]
    columns = flat_rows
    pre_act = jnp.dot(
        columns,
        by_rows(up_local),
        preferred_element_type=jnp.float32,
    )
    hidden = jax.nn.gelu(pre_act + up_bias[0], approximate=False).astype(jnp.bfloat16)
    down_terms = times_columns(hidden, down_weight[0])
    mlp_sum = lax.psum_scatter(
        down_terms.astype(jnp.bfloat16), "lat", scatter_dimension=0, tiled=True
    ).astype(jnp.float32)
    handed_flat = tile_in.reshape(-1, width).astype(jnp.float32) + layer_norm(mlp_sum, mlp_gain[0])
    handed = handed_flat.astype(jnp.bfloat16).reshape(height, breadth, width)
    passed = shifted(handed, "section", 1)
    first_section = lax.axis_index("section") == 0
    entering = jnp.where(first_section, fresh_input, passed)
    shift_lat = offsets[0]
    shift_lon = offsets[1]
    strip_width = W // 2
    after_strip = from_behind(entering[:, :strip_width], "lon", -1)
    rolled = lax.dynamic_slice_in_dim(
        jnp.concatenate([entering, after_strip], 1), shift_lon, breadth, 1
    )
    region_marks = regions.astype(jnp.bfloat16)
    grid, grid_marks = (
        lax.all_gather(rolled, "lat", axis=0, tiled=True),
        lax.all_gather(region_marks, "lat", axis=0, tiled=True),
    )
    grid = jnp.roll(grid, -shift_lat, axis=0)
    grid_height = grid.shape[0]
    flat_grid = grid.reshape(-1, width)
    heads_local = logit_scale.shape[1]
    head_size = qkv_weight.shape[3] // heads_local
    piece = by_rows(qkv_weight[0])
    columns = flat_grid
    packed = jnp.dot(columns, piece.reshape(piece.shape[0], -1), preferred_element_type=jnp.float32)
    packed = packed.astype(jnp.bfloat16).reshape(grid_height, breadth, 3, heads_local, head_size)
    context = attend(packed, grid_marks, logit_scale[0], position_bias[0])
    context = unwindow(context, grid_height, breadth, W).reshape(
        grid_height * breadth, heads_local * head_size
    )
    out_terms = times_columns(context, out_weight[0])
    out_terms = jnp.roll(out_terms.reshape(grid_height, breadth, width), shift_lat, axis=0).reshape(
        -1, width
    )
    attn_sum = lax.psum_scatter(
        out_terms.astype(jnp.bfloat16), "lat", scatter_dimension=0, tiled=True
    ).astype(jnp.float32)
    branch = layer_norm(attn_sum, attn_gain[0]).astype(jnp.bfloat16).reshape(height, breadth, width)
    tail_strip = from_behind(branch[:, -strip_width:], "lon", 1)
    branch = lax.dynamic_slice_in_dim(
        jnp.concatenate([tail_strip, branch], 1), strip_width - shift_lon, breadth, 1
    )
    opened = (entering.astype(jnp.float32) + branch.astype(jnp.float32)).astype(jnp.bfloat16)
    return (handed[None], opened[None])


def solution(mesh):
    return jax.shard_map(
        per_device,
        mesh=mesh,
        in_specs=(
            P("section", ("grp", "lat"), "lon", None),
            P(("grp", "lat"), "lon", None),
            P("grp"),
            P(("grp", "lat"), "lon"),
            P("section", "lon", "lat"),
            P("section", "lat"),
            P("section", "lat", "lon"),
            P("section", None),
            P("section", "lon", None, "lat"),
            P("section", "lat"),
            P("section", "lat", None, None),
            P("section", "lat", "lon"),
            P("section", None),
        ),
        out_specs=(
            P("section", ("grp", "lat"), "lon", None),
            P("section", ("grp", "lat"), "lon", None),
        ),
        check_vma=False,
    )
```

```python
import functools

import jax
import jax.numpy as jnp
from jax import lax
from jax.experimental import pallas as pl
from jax.experimental.pallas import tpu as pltpu
from jax.sharding import PartitionSpec as P

W = 8


def shifted(array, axis, by):
    count = lax.axis_size(axis)
    pairs = [(i, i + by) for i in range(count) if 0 <= i + by < count]
    return lax.ppermute(array, axis, pairs)


def from_behind(block, axis, distance):
    devices = range(lax.axis_size(axis))
    route = [((i - distance) % len(devices), i) for i in devices]
    return lax.ppermute(block, axis, route)


def layer_norm(total, norm_gain):
    mean = jnp.mean(total, axis=-1, keepdims=True)
    centered = total - mean
    variance = jnp.mean(centered * centered, axis=-1, keepdims=True)
    return centered * lax.rsqrt(variance + 1e-05) * norm_gain


def windows(values, side):
    height, breadth = (values.shape[0], values.shape[1])
    rest = values.shape[2:]
    blocks = values.reshape((height // side, side, breadth // side, side) + rest)
    blocks = jnp.moveaxis(blocks, 2, 1)
    return blocks.reshape((-1, side * side) + rest)


def unwindow(values, height, breadth, side):
    rest = values.shape[2:]
    blocks = values.reshape((height // side, breadth // side, side, side) + rest)
    blocks = jnp.moveaxis(blocks, 1, 2)
    return blocks.reshape((height, breadth) + rest)


def attend(packed, region_marks, head_scale, pos_bias):
    blocks = windows(packed, W)
    query_rows = blocks[:, :, 0]
    key_rows = blocks[:, :, 1]
    value_rows = blocks[:, :, 2]
    inner_dot = jnp.einsum(
        "wihd,wjhd->whij", query_rows, key_rows, preferred_element_type=jnp.float32
    )
    query_wide = query_rows.astype(jnp.float32)
    key_wide = key_rows.astype(jnp.float32)
    query_norm = lax.rsqrt(jnp.sum(query_wide * query_wide, axis=-1) + 1e-06)
    key_norm = lax.rsqrt(jnp.sum(key_wide * key_wide, axis=-1) + 1e-06)
    cosine = inner_dot * jnp.transpose(query_norm, (0, 2, 1))[:, :, :, None]
    cosine = cosine * jnp.transpose(key_norm, (0, 2, 1))[:, :, None, :]
    score = cosine * head_scale[None, :, None, None] + pos_bias[None]
    marked = windows(region_marks, W)
    same_region = (marked[:, :, None] == marked[:, None, :])[:, None]
    raw_weights = jnp.where(same_region, jnp.exp(score), jnp.float32(0.0))
    weights = (raw_weights / jnp.sum(raw_weights, axis=-1, keepdims=True)).astype(jnp.bfloat16)
    context = jnp.einsum("whij,wjhd->wihd", weights, value_rows, preferred_element_type=jnp.float32)
    return context.astype(jnp.bfloat16)


MESH = pl.DeviceIdType.MESH
TILE_ROWS = 16
SPLITS = (2, 2, 2, 1)
AHEAD = 2


def relay_kernel(count, *refs):
    kinds = len(SPLITS)
    shards, wholes = refs[:kinds], refs[kinds : 2 * kinds]
    hop_send, hop_recv, side_send, side_recv, own_sem = refs[2 * kinds :]
    place = lax.axis_index("lon")
    half = lax.axis_index("grp")
    pieces = [(kind, part) for kind in range(kinds) for part in range(SPLITS[kind])]

    def rows_of(piece, side):
        kind, part = pieces[piece]
        length = shards[kind].shape[0] // (2 * SPLITS[kind])
        start = pl.multiple_of((side * SPLITS[kind] + part) * length, TILE_ROWS)
        return kind, pl.ds(start, length)

    def hop(piece, way, origin, own):
        kind, rows = rows_of(piece, half)
        target = wholes[kind].at[origin, rows]
        index = 0 if way > 0 else 1
        return pltpu.make_async_remote_copy(
            src_ref=shards[kind].at[rows] if own else target,
            dst_ref=target,
            send_sem=hop_send.at[index, piece, origin],
            recv_sem=hop_recv.at[index, piece, origin],
            device_id={"lon": jnp.clip(place + way, 0, count - 1)},
            device_id_type=MESH,
        )

    def across(piece, origin, side):
        kind, rows = rows_of(piece, side)
        target = wholes[kind].at[origin, rows]
        return pltpu.make_async_remote_copy(
            src_ref=target,
            dst_ref=target,
            send_sem=side_send.at[piece, origin],
            recv_sem=side_recv.at[piece, origin],
            device_id={"grp": 1 - half},
            device_id_type=MESH,
        )

    def has(way):
        return place < count - 1 if way > 0 else place > 0

    barrier = pltpu.get_barrier_semaphore()
    for way in (1, -1):

        @pl.when(has(way))
        def _():
            pl.semaphore_signal(
                barrier, inc=1, device_id={"lon": place + way}, device_id_type=MESH
            )

    pl.semaphore_signal(barrier, inc=1, device_id={"grp": 1 - half}, device_id_type=MESH)
    pl.semaphore_wait(barrier, 1 + jnp.where(has(1), 1, 0) + jnp.where(has(-1), 1, 0))

    def send_own(piece):
        for way in (1, -1):

            @pl.when(has(way))
            def _():
                hop(piece, way, place, True).start()

    for piece in range(AHEAD):
        send_own(piece)
    own = [
        pltpu.make_async_copy(shards[kind], wholes[kind].at[place], own_sem.at[kind])
        for kind in range(kinds)
    ]
    for copy in own:
        copy.start()
    for piece in range(len(pieces)):
        if piece + AHEAD < len(pieces):
            send_own(piece + AHEAD)

        def step(distance, carry):
            for way in (1, -1):
                origin = place - distance * way

                @pl.when((origin >= 0) & (origin < count))
                def _():
                    hop(piece, way, origin, False).wait_recv()

                    @pl.when(has(way))
                    def _():
                        hop(piece, way, origin, False).start()

                    across(piece, origin, half).start()

            return carry

        lax.fori_loop(1, count, step, 0)
    for copy in own:
        copy.wait()
    for piece in range(len(pieces)):

        def drain(origin, carry):
            @pl.when(origin != place)
            def _():
                across(piece, origin, 1 - half).wait_recv()
                across(piece, origin, half).wait_send()

            for way in (1, -1):

                @pl.when(has(way) & ((place - origin) * way >= 0))
                def _():
                    hop(piece, way, origin, False).wait_send()

            return carry

        lax.fori_loop(0, count, drain, 0)


def relayed(shards):
    count = lax.axis_size("lon")
    pieces = sum(SPLITS)
    return pl.pallas_call(
        functools.partial(relay_kernel, count),
        out_shape=[jax.ShapeDtypeStruct((count,) + w.shape, w.dtype) for w in shards],
        in_specs=[pl.BlockSpec(memory_space=pl.ANY)] * len(shards),
        out_specs=[pl.BlockSpec(memory_space=pl.ANY)] * len(shards),
        scratch_shapes=[
            pltpu.SemaphoreType.DMA((2, pieces, count)),
            pltpu.SemaphoreType.DMA((2, pieces, count)),
            pltpu.SemaphoreType.DMA((pieces, count)),
            pltpu.SemaphoreType.DMA((pieces, count)),
            pltpu.SemaphoreType.DMA((len(shards),)),
        ],
        compiler_params=pltpu.CompilerParams(collective_id=0, has_side_effects=True),
    )(*shards)


def gathered_weights(shards):
    fits = all(w.shape[0] % (2 * n * TILE_ROWS) == 0 for w, n in zip(shards, SPLITS))
    if fits and lax.axis_size("grp") == 2:
        return relayed(shards)
    return [lax.all_gather(w, "lon", axis=0, tiled=False) for w in shards]


def by_rows(whole):
    return whole.reshape(-1, whole.shape[2])


def times_columns(left, whole):
    terms = jnp.einsum("th,lhc->tlc", left, whole, preferred_element_type=jnp.float32)
    return terms.reshape(left.shape[0], -1)


def per_device(
    section_input,
    fresh_input,
    offsets,
    regions,
    up_weight,
    up_bias,
    down_weight,
    mlp_gain,
    qkv_weight,
    logit_scale,
    position_bias,
    out_weight,
    attn_gain,
):
    qkv_flat = qkv_weight[0].reshape(qkv_weight.shape[1], -1)
    up_whole, down_whole, qkv_whole, out_whole = gathered_weights(
        [up_weight[0], down_weight[0], qkv_flat, out_weight[0]]
    )
    tile_in = section_input[0]
    height, breadth, width = tile_in.shape
    gathered = lax.all_gather(tile_in, "lat", axis=0, tiled=True)
    flat_rows = gathered.reshape(-1, width)
    columns = flat_rows
    pre_act = jnp.dot(
        columns,
        by_rows(up_whole),
        preferred_element_type=jnp.float32,
    )
    hidden = jax.nn.gelu(pre_act + up_bias[0], approximate=False).astype(jnp.bfloat16)
    down_terms = times_columns(hidden, down_whole)
    mlp_sum = lax.psum_scatter(
        down_terms.astype(jnp.bfloat16), "lat", scatter_dimension=0, tiled=True
    ).astype(jnp.float32)
    handed_flat = tile_in.reshape(-1, width).astype(jnp.float32) + layer_norm(mlp_sum, mlp_gain[0])
    handed = handed_flat.astype(jnp.bfloat16).reshape(height, breadth, width)
    passed = shifted(handed, "section", 1)
    first_section = lax.axis_index("section") == 0
    entering = jnp.where(first_section, fresh_input, passed)
    shift_lat = offsets[0]
    shift_lon = offsets[1]
    strip_width = W // 2
    after_strip = from_behind(entering[:, :strip_width], "lon", -1)
    rolled = lax.dynamic_slice_in_dim(
        jnp.concatenate([entering, after_strip], 1), shift_lon, breadth, 1
    )
    region_marks = regions.astype(jnp.bfloat16)
    grid, grid_marks = (
        lax.all_gather(rolled, "lat", axis=0, tiled=True),
        lax.all_gather(region_marks, "lat", axis=0, tiled=True),
    )
    grid = jnp.roll(grid, -shift_lat, axis=0)
    grid_height = grid.shape[0]
    flat_grid = grid.reshape(-1, width)
    heads_local = logit_scale.shape[1]
    head_size = qkv_weight.shape[3] // heads_local
    columns = flat_grid
    packed = jnp.dot(columns, by_rows(qkv_whole), preferred_element_type=jnp.float32)
    packed = packed.astype(jnp.bfloat16).reshape(grid_height, breadth, 3, heads_local, head_size)
    context = attend(packed, grid_marks, logit_scale[0], position_bias[0])
    context = unwindow(context, grid_height, breadth, W).reshape(
        grid_height * breadth, heads_local * head_size
    )
    out_terms = times_columns(context, out_whole)
    out_terms = jnp.roll(out_terms.reshape(grid_height, breadth, width), shift_lat, axis=0).reshape(
        -1, width
    )
    attn_sum = lax.psum_scatter(
        out_terms.astype(jnp.bfloat16), "lat", scatter_dimension=0, tiled=True
    ).astype(jnp.float32)
    branch = layer_norm(attn_sum, attn_gain[0]).astype(jnp.bfloat16).reshape(height, breadth, width)
    tail_strip = from_behind(branch[:, -strip_width:], "lon", 1)
    branch = lax.dynamic_slice_in_dim(
        jnp.concatenate([tail_strip, branch], 1), strip_width - shift_lon, breadth, 1
    )
    opened = (entering.astype(jnp.float32) + branch.astype(jnp.float32)).astype(jnp.bfloat16)
    return (handed[None], opened[None])


def solution(mesh):
    return jax.shard_map(
        per_device,
        mesh=mesh,
        in_specs=(
            P("section", ("grp", "lat"), "lon", None),
            P(("grp", "lat"), "lon", None),
            P("grp"),
            P(("grp", "lat"), "lon"),
            P("section", "lon", "lat"),
            P("section", "lat"),
            P("section", "lat", "lon"),
            P("section", None),
            P("section", "lon", None, "lat"),
            P("section", "lat"),
            P("section", "lat", None, None),
            P("section", "lat", "lon"),
            P("section", None),
        ),
        out_specs=(
            P("section", ("grp", "lat"), "lon", None),
            P("section", ("grp", "lat"), "lon", None),
        ),
        check_vma=False,
    )
```

```python
import functools

import jax
import jax.numpy as jnp
from jax import lax
from jax.experimental import pallas as pl
from jax.experimental.pallas import tpu as pltpu
from jax.sharding import PartitionSpec as P

W = 8


def shifted(array, axis, by):
    count = lax.axis_size(axis)
    pairs = [(i, i + by) for i in range(count) if 0 <= i + by < count]
    return lax.ppermute(array, axis, pairs)


def from_behind(block, axis, distance):
    devices = range(lax.axis_size(axis))
    route = [((i - distance) % len(devices), i) for i in devices]
    return lax.ppermute(block, axis, route)


def layer_norm(total, norm_gain):
    mean = jnp.mean(total, axis=-1, keepdims=True)
    centered = total - mean
    variance = jnp.mean(centered * centered, axis=-1, keepdims=True)
    return centered * lax.rsqrt(variance + 1e-05) * norm_gain


def windows(values, side):
    height, breadth = (values.shape[0], values.shape[1])
    rest = values.shape[2:]
    blocks = values.reshape((height // side, side, breadth // side, side) + rest)
    blocks = jnp.moveaxis(blocks, 2, 1)
    return blocks.reshape((-1, side * side) + rest)


def unwindow(values, height, breadth, side):
    rest = values.shape[2:]
    blocks = values.reshape((height // side, breadth // side, side, side) + rest)
    blocks = jnp.moveaxis(blocks, 1, 2)
    return blocks.reshape((height, breadth) + rest)


def attend(packed, region_marks, head_scale, pos_bias):
    query_rows, key_rows, value_rows = [windows(packed[kind], W) for kind in range(3)]
    inner_dot = jnp.einsum(
        "wihd,wjhd->whij", query_rows, key_rows, preferred_element_type=jnp.float32
    )
    query_wide = query_rows.astype(jnp.float32)
    key_wide = key_rows.astype(jnp.float32)
    query_norm = lax.rsqrt(jnp.sum(query_wide * query_wide, axis=-1) + 1e-06)
    key_norm = lax.rsqrt(jnp.sum(key_wide * key_wide, axis=-1) + 1e-06)
    cosine = inner_dot * jnp.transpose(query_norm, (0, 2, 1))[:, :, :, None]
    cosine = cosine * jnp.transpose(key_norm, (0, 2, 1))[:, :, None, :]
    score = cosine * head_scale[None, :, None, None] + pos_bias[None]
    marked = windows(region_marks, W)
    same_region = (marked[:, :, None] == marked[:, None, :])[:, None]
    raw_weights = jnp.where(same_region, jnp.exp(score), jnp.float32(0.0))
    weights = (raw_weights / jnp.sum(raw_weights, axis=-1, keepdims=True)).astype(jnp.bfloat16)
    context = jnp.einsum("whij,wjhd->wihd", weights, value_rows, preferred_element_type=jnp.float32)
    return context.astype(jnp.bfloat16)


MESH = pl.DeviceIdType.MESH
TILE_ROWS = 16
SPLITS = (2, 2, 2, 1)
AHEAD = 3
UP_READY = 3
DOWN_READY = 5
VMEM_BYTES = 40 * 2**20


def relay_kernel(count, sections, *refs):
    kinds = len(SPLITS)
    shards = refs[:kinds]
    tokens, bias, tile, gain, fresh, handed, entering, qkv_whole, out_whole = refs[
        kinds : kinds + 9
    ]
    (
        up_whole,
        down_whole,
        hidden,
        own_terms,
        sent_terms,
        peer_terms,
        hop_send,
        hop_recv,
        side_send,
        side_recv,
        own_sem,
        term_send,
        term_recv,
        hand_sem,
    ) = refs[kinds + 9 :]
    wholes = (up_whole, down_whole, qkv_whole, out_whole)
    place = lax.axis_index("lon")
    half = lax.axis_index("grp")
    row_half = lax.axis_index("lat")
    section = lax.axis_index("section")
    pieces = [(kind, part) for kind in range(kinds) for part in range(SPLITS[kind])]

    def rows_of(piece, side):
        kind, part = pieces[piece]
        length = shards[kind].shape[1] // (2 * SPLITS[kind])
        return kind, (side * SPLITS[kind] + part) * length, length

    def target_of(piece, origin, side):
        kind, start, length = rows_of(piece, side)
        first = pl.multiple_of(origin * shards[kind].shape[1] + start, TILE_ROWS)
        return wholes[kind].at[:, pl.ds(first, length)]

    def hop(piece, way, origin, own):
        kind, start, length = rows_of(piece, half)
        target = target_of(piece, origin, half)
        source = shards[kind].at[:, pl.ds(pl.multiple_of(start, TILE_ROWS), length)]
        index = 0 if way > 0 else 1
        return pltpu.make_async_remote_copy(
            src_ref=source if own else target,
            dst_ref=target,
            send_sem=hop_send.at[index, piece, origin],
            recv_sem=hop_recv.at[index, piece, origin],
            device_id={"lon": jnp.clip(place + way, 0, count - 1)},
            device_id_type=MESH,
        )

    def across(piece, origin, side):
        target = target_of(piece, origin, side)
        return pltpu.make_async_remote_copy(
            src_ref=target,
            dst_ref=target,
            send_sem=side_send.at[piece, origin],
            recv_sem=side_recv.at[piece, origin],
            device_id={"grp": 1 - half},
            device_id_type=MESH,
        )

    def has(way):
        return place < count - 1 if way > 0 else place > 0

    def has_section(way):
        return section < sections - 1 if way > 0 else section > 0

    barrier = pltpu.get_barrier_semaphore()
    for way in (1, -1):

        @pl.when(has(way))
        def _():
            pl.semaphore_signal(
                barrier, inc=1, device_id={"lon": place + way}, device_id_type=MESH
            )

        @pl.when(has_section(way))
        def _():
            pl.semaphore_signal(
                barrier, inc=1, device_id={"section": section + way}, device_id_type=MESH
            )

    pl.semaphore_signal(barrier, inc=1, device_id={"grp": 1 - half}, device_id_type=MESH)
    pl.semaphore_signal(barrier, inc=1, device_id={"lat": 1 - row_half}, device_id_type=MESH)
    greeted = 2
    for way in (1, -1):
        greeted = greeted + jnp.where(has(way), 1, 0) + jnp.where(has_section(way), 1, 0)
    pl.semaphore_wait(barrier, greeted)

    def send_own(piece):
        for way in (1, -1):

            @pl.when(has(way))
            def _():
                hop(piece, way, place, True).start()

    def term_copy():
        return pltpu.make_async_remote_copy(
            src_ref=sent_terms,
            dst_ref=peer_terms,
            send_sem=term_send,
            recv_sem=term_recv,
            device_id={"lat": 1 - row_half},
            device_id_type=MESH,
        )

    def hand_copy():
        return pltpu.make_async_remote_copy(
            src_ref=handed,
            dst_ref=entering,
            send_sem=hand_sem.at[0],
            recv_sem=hand_sem.at[1],
            device_id={"section": jnp.clip(section + 1, 0, sections - 1)},
            device_id_type=MESH,
        )

    def fresh_copy():
        return pltpu.make_async_copy(fresh, entering, hand_sem.at[2])

    def await_across(kind):
        own[kind].wait()
        for piece in range(len(pieces)):
            if pieces[piece][0] == kind:

                def arrive(origin, carry):
                    @pl.when(origin != place)
                    def _():
                        across(piece, origin, 1 - half).wait_recv()

                    return carry

                lax.fori_loop(0, count, arrive, 0)

    def run_up():
        width = hidden.shape[1] // 4

        def block(index, carry):
            columns = pl.ds(pl.multiple_of(index * width, 128), width)
            total = jnp.dot(
                tokens[...], up_whole[0, :, columns], preferred_element_type=jnp.float32
            )
            total = total + bias[:, columns]
            total = 0.5 * total * (1.0 + lax.erf(total * (0.5**0.5)))
            hidden[:, columns] = total.astype(hidden.dtype)
            return carry

        lax.fori_loop(0, 4, block, 0)

    def run_down():
        height = own_terms.shape[0]
        depth, width = shards[1].shape[1:]

        def block(whose, result):
            rows = pl.ds(pl.multiple_of(whose * height, TILE_ROWS), height)
            for origin in range(count):
                term = jnp.dot(
                    hidden[rows, :],
                    down_whole[0, origin * depth : (origin + 1) * depth, :],
                    preferred_element_type=jnp.float32,
                )
                result[:, origin * width : (origin + 1) * width] = term.astype(result.dtype)

        block(1 - row_half, sent_terms)
        term_copy().start()
        block(row_half, own_terms)

    def finish_mlp():
        term_copy().wait_recv()
        total = own_terms[...].astype(jnp.float32) + peer_terms[...].astype(jnp.float32)
        moved = tile[...].astype(jnp.float32) + layer_norm(total, gain[...])
        handed[...] = moved.astype(handed.dtype)

        @pl.when(has_section(1))
        def _():
            hand_copy().start()

    own = [
        pltpu.make_async_copy(
            shards[kind],
            wholes[kind].at[
                :,
                pl.ds(
                    pl.multiple_of(place * shards[kind].shape[1], TILE_ROWS),
                    shards[kind].shape[1],
                ),
            ],
            own_sem.at[kind],
        )
        for kind in range(kinds)
    ]
    for piece in range(AHEAD):
        send_own(piece)
    for copy in own:
        copy.start()

    @pl.when(jnp.logical_not(has_section(-1)))
    def _():
        fresh_copy().start()

    for piece in range(len(pieces)):
        if piece + AHEAD < len(pieces):
            send_own(piece + AHEAD)
        if piece == UP_READY:
            await_across(0)
            run_up()
        if piece == DOWN_READY:
            await_across(1)
            run_down()
        if piece == DOWN_READY + 1:
            finish_mlp()

        def step(distance, carry):
            for way in (1, -1):
                origin = place - distance * way

                @pl.when((origin >= 0) & (origin < count))
                def _():
                    hop(piece, way, origin, False).wait_recv()

                    @pl.when(has(way))
                    def _():
                        hop(piece, way, origin, False).start()

                    across(piece, origin, half).start()

            return carry

        lax.fori_loop(1, count, step, 0)
    await_across(2)
    await_across(3)
    for piece in range(len(pieces)):

        def drain(origin, carry):
            @pl.when(origin != place)
            def _():
                across(piece, origin, half).wait_send()

            for way in (1, -1):

                @pl.when(has(way) & ((place - origin) * way >= 0))
                def _():
                    hop(piece, way, origin, False).wait_send()

            return carry

        lax.fori_loop(0, count, drain, 0)
    term_copy().wait_send()

    @pl.when(has_section(1))
    def _():
        hand_copy().wait_send()

    @pl.when(has_section(-1))
    def _():
        hand_copy().wait_recv()

    @pl.when(jnp.logical_not(has_section(-1)))
    def _():
        fresh_copy().wait()


def relayed(shards, tokens, bias, tile, gain, fresh):
    count = lax.axis_size("lon")
    pieces = sum(SPLITS)
    wholes = [
        jax.ShapeDtypeStruct((w.shape[0], count * w.shape[1], w.shape[2]), w.dtype)
        for w in shards
    ]
    near = pl.BlockSpec(memory_space=pltpu.VMEM)
    far = pl.BlockSpec(memory_space=pl.ANY)
    return pl.pallas_call(
        functools.partial(relay_kernel, count, lax.axis_size("section")),
        out_shape=[jax.ShapeDtypeStruct(tile.shape, tile.dtype)] * 2 + wholes[2:],
        in_specs=[far] * len(shards) + [near] * 4 + [far],
        out_specs=[near, far, far, far],
        scratch_shapes=[
            pltpu.VMEM(wholes[0].shape, wholes[0].dtype),
            pltpu.VMEM(wholes[1].shape, wholes[1].dtype),
            pltpu.VMEM((tokens.shape[0], shards[0].shape[2]), tile.dtype),
            pltpu.VMEM(tile.shape, tile.dtype),
            pltpu.VMEM(tile.shape, tile.dtype),
            pltpu.VMEM(tile.shape, tile.dtype),
            pltpu.SemaphoreType.DMA((2, pieces, count)),
            pltpu.SemaphoreType.DMA((2, pieces, count)),
            pltpu.SemaphoreType.DMA((pieces, count)),
            pltpu.SemaphoreType.DMA((pieces, count)),
            pltpu.SemaphoreType.DMA((len(shards),)),
            pltpu.SemaphoreType.DMA,
            pltpu.SemaphoreType.DMA,
            pltpu.SemaphoreType.DMA((3,)),
        ],
        compiler_params=pltpu.CompilerParams(
            collective_id=0, has_side_effects=True, vmem_limit_bytes=VMEM_BYTES
        ),
    )(*shards, tokens, bias, tile, gain, fresh)


def gathered(shards, tokens, bias, tile, gain, fresh):
    up_whole, down_whole, qkv_whole, out_whole = [
        lax.all_gather(w, "lon", axis=1, tiled=True) for w in shards
    ]
    pre_act = jnp.dot(tokens, up_whole[0], preferred_element_type=jnp.float32)
    hidden = jax.nn.gelu(pre_act + bias, approximate=False).astype(jnp.bfloat16)
    down_terms = times_columns(hidden, down_whole).astype(jnp.bfloat16)
    mlp_sum = lax.psum_scatter(down_terms, "lat", scatter_dimension=0, tiled=True)
    handed = tile.astype(jnp.float32) + layer_norm(mlp_sum.astype(jnp.float32), gain)
    handed = handed.astype(jnp.bfloat16)
    passed = shifted(handed, "section", 1)
    entering = jnp.where(lax.axis_index("section") == 0, fresh, passed)
    return handed, entering, qkv_whole, out_whole


def mlp_and_weights(shards, *rest):
    fits = all(w.shape[1] % (2 * n * TILE_ROWS) == 0 for w, n in zip(shards, SPLITS))
    pairs = lax.axis_size("grp") == 2 and lax.axis_size("lat") == 2
    return relayed(shards, *rest) if fits and pairs else gathered(shards, *rest)


def times_columns(left, whole):
    whole = whole.reshape(lax.axis_size("lon"), -1, whole.shape[2])
    terms = jnp.einsum("th,lhc->tlc", left, whole, preferred_element_type=jnp.float32)
    return terms.reshape(left.shape[0], -1)


def per_device(
    section_input,
    fresh_input,
    offsets,
    regions,
    up_weight,
    up_bias,
    down_weight,
    mlp_gain,
    qkv_weight,
    logit_scale,
    position_bias,
    out_weight,
    attn_gain,
):
    tile_in = section_input[0]
    height, breadth, width = tile_in.shape
    token_rows = lax.all_gather(tile_in, "lat", axis=0, tiled=True).reshape(-1, width)
    handed, entering, qkv_whole, out_whole = mlp_and_weights(
        [up_weight, down_weight, jnp.swapaxes(qkv_weight[0], 0, 1), out_weight],
        token_rows,
        up_bias,
        tile_in.reshape(-1, width),
        mlp_gain,
        fresh_input.reshape(-1, width),
    )
    handed = handed.reshape(height, breadth, width)
    entering = entering.reshape(height, breadth, width)
    shift_lat = offsets[0]
    shift_lon = offsets[1]
    strip_width = W // 2
    after_strip = from_behind(entering[:, :strip_width], "lon", -1)
    rolled = lax.dynamic_slice_in_dim(
        jnp.concatenate([entering, after_strip], 1), shift_lon, breadth, 1
    )
    region_marks = regions.astype(jnp.bfloat16)
    grid, grid_marks = (
        lax.all_gather(rolled, "lat", axis=0, tiled=True),
        lax.all_gather(region_marks, "lat", axis=0, tiled=True),
    )
    grid = jnp.roll(grid, -shift_lat, axis=0)
    grid_height = grid.shape[0]
    flat_grid = grid.reshape(-1, width)
    heads_local = logit_scale.shape[1]
    head_size = qkv_weight.shape[3] // heads_local
    packed = jnp.einsum("td,kdc->ktc", flat_grid, qkv_whole, preferred_element_type=jnp.float32)
    packed = packed.astype(jnp.bfloat16).reshape(3, grid_height, breadth, heads_local, head_size)
    context = attend(packed, grid_marks, logit_scale[0], position_bias[0])
    context = unwindow(context, grid_height, breadth, W).reshape(
        grid_height * breadth, heads_local * head_size
    )
    out_terms = times_columns(context, out_whole)
    out_terms = jnp.roll(out_terms.reshape(grid_height, breadth, width), shift_lat, axis=0).reshape(
        -1, width
    )
    attn_sum = lax.psum_scatter(
        out_terms.astype(jnp.bfloat16), "lat", scatter_dimension=0, tiled=True
    ).astype(jnp.float32)
    branch = layer_norm(attn_sum, attn_gain[0]).astype(jnp.bfloat16).reshape(height, breadth, width)
    tail_strip = from_behind(branch[:, -strip_width:], "lon", 1)
    branch = lax.dynamic_slice_in_dim(
        jnp.concatenate([tail_strip, branch], 1), strip_width - shift_lon, breadth, 1
    )
    opened = (entering.astype(jnp.float32) + branch.astype(jnp.float32)).astype(jnp.bfloat16)
    return (handed[None], opened[None])


def solution(mesh):
    return jax.shard_map(
        per_device,
        mesh=mesh,
        in_specs=(
            P("section", ("grp", "lat"), "lon", None),
            P(("grp", "lat"), "lon", None),
            P("grp"),
            P(("grp", "lat"), "lon"),
            P("section", "lon", "lat"),
            P("section", "lat"),
            P("section", "lat", "lon"),
            P("section", None),
            P("section", "lon", None, "lat"),
            P("section", "lat"),
            P("section", "lat", None, None),
            P("section", "lat", "lon"),
            P("section", None),
        ),
        out_specs=(
            P("section", ("grp", "lat"), "lon", None),
            P("section", ("grp", "lat"), "lon", None),
        ),
        check_vma=False,
    )
```

```python
import functools

import jax
import jax.numpy as jnp
from jax import lax
from jax.experimental import pallas as pl
from jax.experimental.pallas import tpu as pltpu
from jax.sharding import PartitionSpec as P

W = 8


def shifted(array, axis, by):
    count = lax.axis_size(axis)
    pairs = [(i, i + by) for i in range(count) if 0 <= i + by < count]
    return lax.ppermute(array, axis, pairs)


def from_behind(block, axis, distance):
    devices = range(lax.axis_size(axis))
    route = [((i - distance) % len(devices), i) for i in devices]
    return lax.ppermute(block, axis, route)


def turned(grid, first):
    return lax.dynamic_slice_in_dim(jnp.concatenate([grid, grid], 0), first, grid.shape[0], 0)


def summed_over_lat(terms):
    if lax.axis_size("lat") != 2:
        total = lax.psum_scatter(terms, "lat", scatter_dimension=0, tiled=True)
        return total.astype(jnp.float32)
    me = lax.axis_index("lat")
    rows = terms.shape[0] // 2
    kept = lax.dynamic_slice_in_dim(terms, me * rows, rows, 0)
    given = lax.dynamic_slice_in_dim(terms, (1 - me) * rows, rows, 0)
    return kept.astype(jnp.float32) + from_behind(given, "lat", 1).astype(jnp.float32)


def slab_ids(place, count, shift):
    return (place >= count - W).astype(jnp.int32) + (place >= count - shift).astype(jnp.int32)


def layer_norm(total, norm_gain):
    mean = jnp.mean(total, axis=-1, keepdims=True)
    centered = total - mean
    variance = jnp.mean(centered * centered, axis=-1, keepdims=True)
    return centered * lax.rsqrt(variance + 1e-05) * norm_gain


def windows(values, side):
    height, breadth = (values.shape[0], values.shape[1])
    rest = values.shape[2:]
    blocks = values.reshape((height // side, side, breadth // side, side) + rest)
    blocks = jnp.moveaxis(blocks, 2, 1)
    return blocks.reshape((-1, side * side) + rest)


def unwindow(values, height, breadth, side):
    rest = values.shape[2:]
    blocks = values.reshape((height // side, breadth // side, side, side) + rest)
    blocks = jnp.moveaxis(blocks, 1, 2)
    return blocks.reshape((height, breadth) + rest)


def attend(packed, region_marks, head_scale, pos_bias):
    query_rows, key_rows, value_rows = [windows(packed[kind], W) for kind in range(3)]
    inner_dot = jnp.einsum(
        "wihd,wjhd->whij", query_rows, key_rows, preferred_element_type=jnp.float32
    )
    query_wide = query_rows.astype(jnp.float32)
    key_wide = key_rows.astype(jnp.float32)
    query_norm = lax.rsqrt(jnp.sum(query_wide * query_wide, axis=-1) + 1e-06)
    key_norm = lax.rsqrt(jnp.sum(key_wide * key_wide, axis=-1) + 1e-06)
    cosine = inner_dot * jnp.transpose(query_norm, (0, 2, 1))[:, :, :, None]
    cosine = cosine * jnp.transpose(key_norm, (0, 2, 1))[:, :, None, :]
    score = cosine * head_scale[None, :, None, None] + pos_bias[None]
    marked = windows(region_marks, W)
    same_region = (marked[:, :, None] == marked[:, None, :])[:, None]
    raw_weights = jnp.where(same_region, jnp.exp(score), jnp.float32(0.0))
    weights = (raw_weights / jnp.sum(raw_weights, axis=-1, keepdims=True)).astype(jnp.bfloat16)
    context = jnp.einsum("whij,wjhd->wihd", weights, value_rows, preferred_element_type=jnp.float32)
    return context.astype(jnp.bfloat16)


MESH = pl.DeviceIdType.MESH
TILE_ROWS = 16
SPLITS = (2, 2, 3, 1)
AHEAD = 3
UP_READY = 3
DOWN_READY = 5
VMEM_BYTES = 60 * 2**20
BLOCK = 256


def relay_kernel(count, sections, *refs):
    kinds = len(SPLITS)
    shards = refs[:kinds]
    bias, tile, gain, fresh, handed, entering, qkv_whole, out_whole = refs[kinds : kinds + 8]
    (
        up_whole,
        down_whole,
        hidden,
        own_terms,
        sent_terms,
        peer_terms,
        tokens,
        mate_tokens,
        mate_sent,
        mate_terms,
        hop_send,
        hop_recv,
        side_send,
        side_recv,
        own_sem,
        term_send,
        term_recv,
        hand_sem,
        far_send,
        mate_sem,
    ) = refs[kinds + 8 :]
    wholes = (up_whole, down_whole, qkv_whole, out_whole)
    place = lax.axis_index("lon")
    half = lax.axis_index("grp")
    row_half = lax.axis_index("lat")
    section = lax.axis_index("section")
    parity = lax.rem(place, 2)
    mate = place + 1 - 2 * parity
    units = up_whole.shape[2]
    pieces = [(kind, part) for kind in range(kinds) for part in range(SPLITS[kind])]

    def extent(kind):
        return wholes[kind].shape[1] // count

    def rows_of(piece, side):
        kind, part = pieces[piece]
        length = extent(kind) // (2 * SPLITS[kind])
        return kind, (side * SPLITS[kind] + part) * length, length

    def source_of(kind, start, length, taker):
        if kind == 0:
            columns = pl.ds(pl.multiple_of(taker * units, 128), units)
            return shards[0].at[:, pl.ds(pl.multiple_of(start, TILE_ROWS), length), columns]
        if kind == 1:
            start = taker * units + start
        return shards[kind].at[:, pl.ds(pl.multiple_of(start, TILE_ROWS), length)]

    def target_of(piece, origin, side):
        kind, start, length = rows_of(piece, side)
        first = pl.multiple_of(origin * extent(kind) + start, TILE_ROWS)
        return wholes[kind].at[:, pl.ds(first, length)]

    def hop(piece, way, origin, own, stride):
        kind, start, length = rows_of(piece, half)
        target = target_of(piece, origin, half)
        index = 0 if way > 0 else 1
        if own:
            source = source_of(kind, start, length, lax.rem(place + stride, 2))
        else:
            source = target
        far_own = own and stride == 2
        return pltpu.make_async_remote_copy(
            src_ref=source,
            dst_ref=target,
            send_sem=far_send.at[index, piece] if far_own else hop_send.at[index, piece, origin],
            recv_sem=hop_recv.at[index, piece, origin],
            device_id={"lon": jnp.clip(place + way * stride, 0, count - 1)},
            device_id_type=MESH,
        )

    def across(piece, origin, side):
        target = target_of(piece, origin, side)
        return pltpu.make_async_remote_copy(
            src_ref=target,
            dst_ref=target,
            send_sem=side_send.at[piece, origin],
            recv_sem=side_recv.at[piece, origin],
            device_id={"grp": 1 - half},
            device_id_type=MESH,
        )

    def has(way, stride=1):
        return place < count - stride if way > 0 else place >= stride

    def strides(piece):
        return (1, 2) if pieces[piece][0] < 2 else (1,)

    def has_section(way):
        return section < sections - 1 if way > 0 else section > 0

    barrier = pltpu.get_barrier_semaphore()
    for way in (1, -1):

        for stride in (1, 2):

            @pl.when(has(way, stride))
            def _():
                pl.semaphore_signal(
                    barrier, inc=1, device_id={"lon": place + way * stride}, device_id_type=MESH
                )

        @pl.when(has_section(way))
        def _():
            pl.semaphore_signal(
                barrier, inc=1, device_id={"section": section + way}, device_id_type=MESH
            )

    pl.semaphore_signal(barrier, inc=1, device_id={"grp": 1 - half}, device_id_type=MESH)
    pl.semaphore_signal(barrier, inc=1, device_id={"lat": 1 - row_half}, device_id_type=MESH)
    greeted = 2
    for way in (1, -1):
        greeted = greeted + jnp.where(has(way), 1, 0) + jnp.where(has(way, 2), 1, 0)
        greeted = greeted + jnp.where(has_section(way), 1, 0)
    pl.semaphore_wait(barrier, greeted)

    def send_own(piece):
        for way in (1, -1):
            for stride in strides(piece):

                @pl.when(has(way, stride))
                def _():
                    hop(piece, way, place, True, stride).start()

    def term_copy():
        return pltpu.make_async_remote_copy(
            src_ref=sent_terms,
            dst_ref=peer_terms,
            send_sem=term_send,
            recv_sem=term_recv,
            device_id={"lat": 1 - row_half},
            device_id_type=MESH,
        )

    def hand_copy():
        return pltpu.make_async_remote_copy(
            src_ref=handed,
            dst_ref=entering,
            send_sem=hand_sem.at[0],
            recv_sem=hand_sem.at[1],
            device_id={"section": jnp.clip(section + 1, 0, sections - 1)},
            device_id_type=MESH,
        )

    def fresh_copy():
        return pltpu.make_async_copy(fresh, entering, hand_sem.at[2])

    def await_across(kind):
        own[kind].wait()
        for piece in range(len(pieces)):
            if pieces[piece][0] == kind:

                def arrive(origin, carry):
                    @pl.when(origin != place)
                    def _():
                        across(piece, origin, 1 - half).wait_recv()

                    return carry

                lax.fori_loop(0, count, arrive, 0)

    tile_rows = tile.shape[0]

    def mate_copy(number, source, target):
        return pltpu.make_async_remote_copy(
            src_ref=source,
            dst_ref=target,
            send_sem=mate_sem.at[number, 0],
            recv_sem=mate_sem.at[number, 1],
            device_id={"lon": mate},
            device_id_type=MESH,
        )

    def slot_rows(whose):
        return pl.ds(pl.multiple_of(whose * tile_rows, TILE_ROWS), tile_rows)

    def tile_slot(whose):
        return mate_tokens.at[slot_rows(whose)]

    def twin_copy(whose):
        return pltpu.make_async_remote_copy(
            src_ref=tile,
            dst_ref=tokens.at[slot_rows(whose)],
            send_sem=mate_sem.at[3, 0],
            recv_sem=mate_sem.at[3, 1],
            device_id={"lat": 1 - row_half},
            device_id_type=MESH,
        )

    def tile_copy():
        return mate_copy(0, tile, tile_slot(row_half))

    def sum_copy():
        return mate_copy(1, mate_sent, mate_terms)

    def share_copy(whose):
        return pltpu.make_async_remote_copy(
            src_ref=tile_slot(whose),
            dst_ref=tile_slot(whose),
            send_sem=mate_sem.at[2, 0],
            recv_sem=mate_sem.at[2, 1],
            device_id={"lat": 1 - row_half},
            device_id_type=MESH,
        )

    def run_up():
        twin_copy(1 - row_half).wait_recv()
        share_copy(1 - row_half).wait_recv()
        share_copy(row_half).wait_send()

        def block(index, carry):
            columns = pl.ds(pl.multiple_of(index * BLOCK, 128), BLOCK)
            biases = bias[:, pl.ds(pl.multiple_of(parity * units + index * BLOCK, 128), BLOCK)]
            for group, rows in enumerate((mate_tokens, tokens)):
                total = jnp.dot(
                    rows[...], up_whole[0, :, columns], preferred_element_type=jnp.float32
                )
                total = total + biases
                total = 0.5 * total * (1.0 + lax.erf(total * (0.5**0.5)))
                hidden[group, :, columns] = total.astype(hidden.dtype)
            return carry

        lax.fori_loop(0, units // BLOCK, block, 0)

    def run_down():
        width = down_whole.shape[2]

        def block(whose, result):
            rows = pl.ds(pl.multiple_of(whose * tile_rows, TILE_ROWS), tile_rows)
            for group in range(2):
                for origin in range(count):
                    term = jnp.dot(
                        hidden[group, rows, :],
                        down_whole[0, origin * units : (origin + 1) * units, :],
                        preferred_element_type=jnp.float32,
                    )
                    result[group, :, origin * width : (origin + 1) * width] = term.astype(
                        result.dtype
                    )

        block(1 - row_half, sent_terms)
        term_copy().start()
        block(row_half, own_terms)

    def lat_sum(group):
        return own_terms[group].astype(jnp.float32) + peer_terms[group].astype(jnp.float32)

    def send_mate_sum():
        term_copy().wait_recv()
        mate_sent[...] = lat_sum(0).astype(mate_sent.dtype)
        sum_copy().start()

    def finish_mlp():
        sum_copy().wait_recv()
        total = lat_sum(1) + mate_terms[...].astype(jnp.float32)
        moved = tile[...].astype(jnp.float32) + layer_norm(total, gain[...])
        handed[...] = moved.astype(handed.dtype)

        @pl.when(has_section(1))
        def _():
            hand_copy().start()

    own = [
        pltpu.make_async_copy(
            source_of(kind, 0, extent(kind), parity),
            wholes[kind].at[
                :, pl.ds(pl.multiple_of(place * extent(kind), TILE_ROWS), extent(kind))
            ],
            own_sem.at[kind],
        )
        for kind in range(kinds)
    ]
    tile_copy().start()
    twin_copy(row_half).start()
    tokens[slot_rows(row_half), :] = tile[...]
    for piece in range(AHEAD):
        send_own(piece)
    for copy in own:
        copy.start()

    @pl.when(jnp.logical_not(has_section(-1)))
    def _():
        fresh_copy().start()

    for piece in range(len(pieces)):
        if piece + AHEAD < len(pieces):
            send_own(piece + AHEAD)
        if piece == UP_READY:
            await_across(0)
            run_up()
        if piece == DOWN_READY:
            await_across(1)
            run_down()
        if piece == DOWN_READY + 1:
            send_mate_sum()
        if piece == DOWN_READY + 2:
            finish_mlp()
        if piece == 1:
            tile_copy().wait_recv()
            share_copy(row_half).start()

        def step(distance, carry):
            for way in (1, -1):
                origin = place - distance * way

                @pl.when((origin >= 0) & (origin < count))
                def _():
                    stride = strides(piece)[-1]
                    hop(piece, way, origin, False, stride).wait_recv()

                    @pl.when(has(way, stride))
                    def _():
                        hop(piece, way, origin, False, stride).start()

                    across(piece, origin, half).start()

            return carry

        lax.fori_loop(1, count, step, 0)
    await_across(2)
    await_across(3)
    for piece in range(len(pieces)):

        def drain(origin, carry):
            @pl.when(origin != place)
            def _():
                across(piece, origin, half).wait_send()

            for way in (1, -1):

                stride = strides(piece)[-1]

                @pl.when(has(way, stride) & ((place - origin) * way > 0))
                def _():
                    hop(piece, way, origin, False, stride).wait_send()

            return carry

        lax.fori_loop(0, count, drain, 0)
        for way in (1, -1):
            for stride in strides(piece):

                @pl.when(has(way, stride))
                def _():
                    hop(piece, way, place, True, stride).wait_send()

    term_copy().wait_send()
    tile_copy().wait_send()
    twin_copy(row_half).wait_send()
    sum_copy().wait_send()

    @pl.when(has_section(1))
    def _():
        hand_copy().wait_send()

    @pl.when(has_section(-1))
    def _():
        hand_copy().wait_recv()

    @pl.when(jnp.logical_not(has_section(-1)))
    def _():
        fresh_copy().wait()


def relayed(shards, bias, tile, gain, fresh):
    count = lax.axis_size("lon")
    pieces = sum(SPLITS)
    wholes = [
        jax.ShapeDtypeStruct((w.shape[0], count * w.shape[1], w.shape[2]), w.dtype)
        for w in shards
    ]
    units = shards[0].shape[2] // 2
    up_shape = wholes[0].shape[:2] + (units,)
    down_shape = (1, count * units, shards[1].shape[2])
    pair_shape = (2 * tile.shape[0], tile.shape[1])
    near = pl.BlockSpec(memory_space=pltpu.VMEM)
    far = pl.BlockSpec(memory_space=pl.ANY)
    return pl.pallas_call(
        functools.partial(relay_kernel, count, lax.axis_size("section")),
        out_shape=[jax.ShapeDtypeStruct(tile.shape, tile.dtype)] * 2 + wholes[2:],
        in_specs=[far] * len(shards) + [near] * 3 + [far],
        out_specs=[near, far, far, far],
        scratch_shapes=[
            pltpu.VMEM(up_shape, wholes[0].dtype),
            pltpu.VMEM(down_shape, wholes[1].dtype),
            pltpu.VMEM((2, pair_shape[0], units), tile.dtype),
            pltpu.VMEM((2,) + tile.shape, tile.dtype),
            pltpu.VMEM((2,) + tile.shape, tile.dtype),
            pltpu.VMEM((2,) + tile.shape, tile.dtype),
            pltpu.VMEM(pair_shape, tile.dtype),
            pltpu.VMEM(pair_shape, tile.dtype),
            pltpu.VMEM(tile.shape, tile.dtype),
            pltpu.VMEM(tile.shape, tile.dtype),
            pltpu.SemaphoreType.DMA((2, pieces, count)),
            pltpu.SemaphoreType.DMA((2, pieces, count)),
            pltpu.SemaphoreType.DMA((pieces, count)),
            pltpu.SemaphoreType.DMA((pieces, count)),
            pltpu.SemaphoreType.DMA((len(shards),)),
            pltpu.SemaphoreType.DMA,
            pltpu.SemaphoreType.DMA,
            pltpu.SemaphoreType.DMA((3,)),
            pltpu.SemaphoreType.DMA((2, pieces)),
            pltpu.SemaphoreType.DMA((4, 2)),
        ],
        compiler_params=pltpu.CompilerParams(
            collective_id=0, has_side_effects=True, vmem_limit_bytes=VMEM_BYTES
        ),
    )(*shards, bias, tile, gain, fresh)


def gathered(shards, bias, tile, gain, fresh):
    tokens = lax.all_gather(tile, "lat", axis=0, tiled=True)
    up_whole, down_whole, qkv_whole, out_whole = [
        lax.all_gather(w, "lon", axis=1, tiled=True) for w in shards
    ]
    pre_act = jnp.dot(tokens, up_whole[0], preferred_element_type=jnp.float32)
    hidden = jax.nn.gelu(pre_act + bias, approximate=False).astype(jnp.bfloat16)
    down_terms = times_columns(hidden, down_whole).astype(jnp.bfloat16)
    handed = tile.astype(jnp.float32) + layer_norm(summed_over_lat(down_terms), gain)
    handed = handed.astype(jnp.bfloat16)
    passed = shifted(handed, "section", 1)
    entering = jnp.where(lax.axis_index("section") == 0, fresh, passed)
    return handed, entering, qkv_whole, out_whole


def mlp_and_weights(shards, *rest):
    fits = all(w.shape[1] % (2 * n * TILE_ROWS) == 0 for w, n in zip(shards, SPLITS))
    fits = fits and shards[1].shape[1] % (4 * SPLITS[1] * TILE_ROWS) == 0
    fits = fits and shards[0].shape[2] % (2 * BLOCK) == 0 and lax.axis_size("lon") % 2 == 0
    pairs = lax.axis_size("grp") == 2 and lax.axis_size("lat") == 2
    return relayed(shards, *rest) if fits and pairs else gathered(shards, *rest)


def times_columns(left, whole):
    whole = whole.reshape(lax.axis_size("lon"), -1, whole.shape[2])
    terms = jnp.einsum("th,lhc->tlc", left, whole, preferred_element_type=jnp.float32)
    return terms.reshape(left.shape[0], -1)


def per_device(
    section_input,
    fresh_input,
    offsets,
    regions,
    up_weight,
    up_bias,
    down_weight,
    mlp_gain,
    qkv_weight,
    logit_scale,
    position_bias,
    out_weight,
    attn_gain,
):
    tile_in = section_input[0]
    height, breadth, width = tile_in.shape
    handed, entering, qkv_whole, out_whole = mlp_and_weights(
        [up_weight, down_weight, jnp.swapaxes(qkv_weight[0], 0, 1), out_weight],
        up_bias,
        tile_in.reshape(-1, width),
        mlp_gain,
        fresh_input.reshape(-1, width),
    )
    handed = handed.reshape(height, breadth, width)
    entering = entering.reshape(height, breadth, width)
    shift_lat = offsets[0]
    shift_lon = offsets[1]
    strip_width = W // 2
    after_strip = from_behind(entering[:, :strip_width], "lon", -1)
    rolled = lax.dynamic_slice_in_dim(
        jnp.concatenate([entering, after_strip], 1), shift_lon, breadth, 1
    )
    grid = lax.all_gather(rolled, "lat", axis=0, tiled=True)
    all_columns = breadth * lax.axis_size("lon")
    own_columns = lax.axis_index("lon") * breadth + jnp.arange(breadth)
    row_slabs = slab_ids(jnp.arange(grid.shape[0]), grid.shape[0], shift_lat)
    column_slabs = slab_ids(own_columns, all_columns, shift_lon)
    grid_marks = 3 * row_slabs[:, None] + column_slabs[None, :]
    grid = turned(grid, shift_lat)
    grid_height = grid.shape[0]
    flat_grid = grid.reshape(-1, width)
    heads_local = logit_scale.shape[1]
    head_size = qkv_weight.shape[3] // heads_local
    packed = jnp.einsum("td,kdc->ktc", flat_grid, qkv_whole, preferred_element_type=jnp.float32)
    packed = packed.astype(jnp.bfloat16).reshape(3, grid_height, breadth, heads_local, head_size)
    context = attend(packed, grid_marks, logit_scale[0], position_bias[0])
    context = unwindow(context, grid_height, breadth, W).reshape(
        grid_height * breadth, heads_local * head_size
    )
    out_terms = times_columns(context, out_whole)
    out_terms = out_terms.astype(jnp.bfloat16).reshape(grid_height, breadth, width)
    out_terms = turned(out_terms, grid_height - shift_lat).reshape(-1, width)
    attn_sum = summed_over_lat(out_terms)
    branch = layer_norm(attn_sum, attn_gain[0]).astype(jnp.bfloat16).reshape(height, breadth, width)
    tail_strip = from_behind(branch[:, -strip_width:], "lon", 1)
    branch = lax.dynamic_slice_in_dim(
        jnp.concatenate([tail_strip, branch], 1), strip_width - shift_lon, breadth, 1
    )
    opened = (entering.astype(jnp.float32) + branch.astype(jnp.float32)).astype(jnp.bfloat16)
    return (handed[None], opened[None])


def solution(mesh):
    return jax.shard_map(
        per_device,
        mesh=mesh,
        in_specs=(
            P("section", ("grp", "lat"), "lon", None),
            P(("grp", "lat"), "lon", None),
            P("grp"),
            P(("grp", "lat"), "lon"),
            P("section", "lon", "lat"),
            P("section", "lat"),
            P("section", "lat", "lon"),
            P("section", None),
            P("section", "lon", None, "lat"),
            P("section", "lat"),
            P("section", "lat", None, None),
            P("section", "lat", "lon"),
            P("section", None),
        ),
        out_specs=(
            P("section", ("grp", "lat"), "lon", None),
            P("section", ("grp", "lat"), "lon", None),
        ),
        check_vma=False,
    )
```
